32 devices in a mesh: tile: 8 (over z, y), sta: 4 (over x, core).
Axes of the slice: x: 2, y: 2, z: 4, core: 2. Of those that a mesh axis runs over, the one named last changes fastest.
Arguments:
- waves: bfloat16 [128, 64, 3, 512], P('sta', 'tile'), may hold values from -256 to 256
- valid: int32 [128, 64], P('sta', 'tile'), may hold values 0 or 1
- station_group: int32 [128], P('sta'), may hold values from 0 to 7, as said below
- owners: int32 [4], replicated, may hold values from 0 to 7, as said below
Outputs:
- peak: float32 [8, 32, 64], P(None, None, 'tile')
The draws below stay inside these ranges and needn't reach their ends.
Inputs may be any that keep to these rules, and one draw needn't show every extreme that they name: `station_group`: every subnetwork holds exactly 16 stations. `owners`: distinct numbers of blocks of 8 consecutive catalog events; the last block is always among them.
All inputs are finite; a program needn't handle non-finite values. No bound on the sum of `valid` on one device may be relied on, other than what follows from the above.
Results may differ from the reference program's by a relative error of at most 0.00037.
Values may be sent and summed in bfloat16 or wider, within the bound.
A program may use at most 64 MiB of HBM per device.

```python
import math
import jax
import jax.numpy as jnp
from jax import lax

STATIONS = 128
SAMPLES = 512
LAGS = 64
GROUPS = 8
EV_DEV = 8
QB = 4
EVENTS = 64


family_total = 12


def draw_waves(key, part):
    key = jax.random.fold_in(key, 17)
    keys = jax.random.split(key, 7)
    family = jax.random.randint(keys[0], (EVENTS,), 0, family_total)
    delays = jax.random.randint(keys[1], (EVENTS,), 0, LAGS // 2 + LAGS // 4)
    record = SAMPLES + LAGS
    template = jax.random.truncated_normal(keys[2], -4.0, 4.0, (STATIONS, family_total, 3, record), jnp.float32)
    envelope = jnp.exp(jax.random.uniform(keys[3], (STATIONS, family_total, 1, record), jnp.float32) * math.log(10.0))
    template = template * envelope

    def station_signal(station_template):

        def event_signal(family_id, delay_one):
            chosen = lax.dynamic_index_in_dim(station_template, family_id, 0, keepdims=False)
            return lax.dynamic_slice_in_dim(chosen, delay_one, SAMPLES, 1)
        return jax.vmap(event_signal)(family, delays)
    signal = lax.map(station_signal, template)
    noise = jax.random.truncated_normal(keys[4], -4.0, 4.0, (STATIONS, EVENTS, 3, SAMPLES), jnp.float32)
    level = jax.random.uniform(keys[5], (STATIONS, EVENTS, 1, 1), jnp.float32, 0.3, 1.2)
    factor = jnp.exp(jax.random.uniform(keys[6], (STATIONS, EVENTS, 1, 1), jnp.float32) * math.log(10.0)) * 0.3
    result = factor * (signal + 4.6 * level * noise)
    return result.astype(jnp.bfloat16)


def draw_station_group(key, part):
    key = jax.random.fold_in(key, 29)
    return (jax.random.permutation(key, STATIONS) % GROUPS).astype(jnp.int32)


def draw_owners(key, part):
    key = jax.random.fold_in(key, 41)
    keys = jax.random.split(key, 2)
    block_total = EVENTS // EV_DEV
    others = jax.random.permutation(keys[0], block_total - 1)[:QB - 1].astype(jnp.int32)
    listed = jnp.concatenate([others, jnp.full((1,), block_total - 1, jnp.int32)])
    order = jax.random.permutation(keys[1], QB)
    return listed[order].astype(jnp.int32)


def with_ends(entries, own_key, low, high):
    extent = entries.shape
    spot = [jax.random.randint(jax.random.fold_in(own_key, axis), (), 0, extent[axis]) for axis in range(len(extent))]
    entries = entries.at[tuple(spot)].set(low)
    longest = extent.index(max(extent))
    spot[longest] = (spot[longest] + 1) % extent[longest]
    return entries.at[tuple(spot)].set(high)


def setup_inputs(seed: int = 0) -> dict:
    splits = jax.random.split(jax.random.key(seed), 5)
    waves = draw_waves(jax.random.fold_in(splits[4], 71), 0)
    valid = with_ends((jax.random.randint(splits[1], (STATIONS, EVENTS), 0, 2) < 1).astype(jnp.int32), jax.random.fold_in(splits[1], 1), 0, 1)
    station_group = draw_station_group(jax.random.fold_in(splits[4], 71), 0)
    owners = draw_owners(jax.random.fold_in(splits[4], 71), 0)
    return dict(waves=waves, valid=valid, station_group=station_group, owners=owners)


epsilon = 1e-06

def normalize(raw_block, mask_block):
    signal = raw_block.astype(jnp.float32)
    inverse_rms = lax.rsqrt(lax.optimization_barrier(jnp.mean(signal * signal, axis=-1, keepdims=True)) + epsilon)
    return (signal * inverse_rms * mask_block[:, :, None, None].astype(jnp.float32)).astype(jnp.bfloat16)

def reference(waves, valid, station_group, owners):
    query_events = (owners[:, None] * EV_DEV + jnp.arange(EV_DEV, dtype=jnp.int32)[None, :]).reshape(-1).astype(jnp.int32)
    query_count = query_events.shape[0]
    query_valid = jnp.take(valid, query_events, axis=1)
    query_waves = normalize(jnp.take(waves, query_events, axis=1), query_valid)
    onehot = (station_group[:, None] == jnp.arange(GROUPS, dtype=jnp.int32)[None, :]).astype(jnp.float32)
    common = jnp.einsum('sg,sq,se->gqe', onehot, query_valid.astype(jnp.float32), valid.astype(jnp.float32), precision=lax.Precision.HIGHEST)
    sorted_order = jnp.argsort(station_group, stable=True).astype(jnp.int32)
    members = sorted_order.reshape(GROUPS, STATIONS // GROUPS)
    fft_length = 2 * SAMPLES
    half_lags = LAGS // 2
    query_spectra = jnp.fft.rfft(query_waves.astype(jnp.float32), n=fft_length, axis=-1)
    block_rows = math.gcd(EVENTS, 128)
    block_count = EVENTS // block_rows

    def block_peaks(block_index):
        first_row = (block_index * block_rows).astype(jnp.int32)
        raw_block = lax.dynamic_slice_in_dim(waves, first_row, block_rows, axis=1)
        mask_block = lax.dynamic_slice_in_dim(valid, first_row, block_rows, axis=1)
        normed = normalize(raw_block, mask_block)
        spectra = jnp.conj(jnp.fft.rfft(normed.astype(jnp.float32), n=fft_length, axis=-1))

        def group_peak(group_index):
            chosen = members[group_index]
            station_spectra = jnp.take(spectra, chosen, axis=0)
            query_group = jnp.take(query_spectra, chosen, axis=0)
            cross_sum = jnp.einsum('sbcf,sqcf->qbf', station_spectra, query_group)
            circular = jnp.fft.irfft(cross_sum, n=fft_length, axis=-1)
            lagged = jnp.concatenate([circular[..., fft_length - half_lags:], circular[..., :half_lags]], axis=-1)
            return lax.optimization_barrier(jnp.max(lagged, axis=-1))
        return lax.map(group_peak, jnp.arange(GROUPS, dtype=jnp.int32))
    peaks = lax.map(block_peaks, jnp.arange(block_count, dtype=jnp.int32))
    peaks = peaks.transpose(1, 2, 0, 3).reshape(GROUPS, query_count, EVENTS)
    return peaks / (SAMPLES * jnp.maximum(common, 1.0))
```

```python
import functools

import jax
import jax.numpy as jnp
from jax import lax
from jax.experimental import pallas as pl
from jax.experimental.pallas import tpu as pltpu
from jax.sharding import PartitionSpec as P

LAGS = 64
GROUPS = 8
PAIR = 2
CHUNK = 2
epsilon = 1e-06
MESH = pl.DeviceIdType.MESH
VMEM_LIMIT = 56 * 1024 * 1024


def normalize(raw_block, mask_block):
    signal = raw_block.astype(jnp.float32)
    inverse_rms = lax.rsqrt(jnp.mean(signal * signal, axis=-1, keepdims=True) + epsilon)
    return (signal * inverse_rms * mask_block[:, :, None, None].astype(jnp.float32)).astype(
        jnp.bfloat16
    )


def spread_kernel(
    line, slots, owners_ref, mine_ref, out_ref,
    beside, up_out, up_in, down_out, down_in,
    beside_send, beside_recv, up_send, up_recv, down_send, down_recv, out_send, out_recv,
):
    tile, sta = lax.axis_index("tile"), lax.axis_index("sta")
    layer, side = tile // 2, tile % 2
    other = layer * 2 + (1 - side)
    half = mine_ref.shape[0] // 2
    steps = half // CHUNK
    above, below = layer * 2 + 2 + side, layer * 2 - 2 + side
    has_above, has_below = layer < line - 1, layer > 0

    barrier = pltpu.get_barrier_semaphore()
    pl.semaphore_signal(barrier, inc=1, device_id=(other, sta), device_id_type=MESH)

    @pl.when(has_above)
    def _():
        pl.semaphore_signal(barrier, inc=1, device_id=(above, sta), device_id_type=MESH)

    @pl.when(has_below)
    def _():
        pl.semaphore_signal(barrier, inc=1, device_id=(below, sta), device_id_type=MESH)

    pl.semaphore_wait(
        barrier, 1 + has_above.astype(jnp.int32) + has_below.astype(jnp.int32)
    )

    def beside_copy(step):
        return pltpu.make_async_remote_copy(
            src_ref=mine_ref.at[pl.ds((1 - side) * half + step * CHUNK, CHUNK)],
            dst_ref=beside.at[step],
            send_sem=beside_send.at[step], recv_sem=beside_recv.at[step],
            device_id=(other, sta), device_id_type=MESH,
        )

    def up_copy(step):
        return pltpu.make_async_remote_copy(
            src_ref=up_out.at[step], dst_ref=up_in.at[step],
            send_sem=up_send.at[step], recv_sem=up_recv.at[step],
            device_id=(above, sta), device_id_type=MESH,
        )

    def down_copy(step):
        return pltpu.make_async_remote_copy(
            src_ref=down_out.at[step], dst_ref=down_in.at[step],
            send_sem=down_send.at[step], recv_sem=down_recv.at[step],
            device_id=(below, sta), device_id_type=MESH,
        )

    def out_copy(step, of_side):
        rows = pl.ds(of_side * half + step * CHUNK, CHUNK)
        return pltpu.make_async_remote_copy(
            src_ref=out_ref.at[:, rows], dst_ref=out_ref.at[:, rows],
            send_sem=out_send.at[step], recv_sem=out_recv.at[step],
            device_id=(other, sta), device_id_type=MESH,
        )

    def each(count, body):
        def run(index, carry):
            body(index)
            return carry

        lax.fori_loop(0, count, run, 0)

    each(steps, lambda step: beside_copy(step).start())
    own = [owners_ref[slot] == tile for slot in range(slots)]
    near = [owners_ref[slot] == other for slot in range(slots)]
    lower = [owners_ref[slot] < layer * 2 for slot in range(slots)]

    def merged(step, slot, passing):
        local = mine_ref[pl.ds(side * half + step * CHUNK, CHUNK)]
        return jnp.where(own[slot], local, jnp.where(near[slot], beside[step], passing))

    lag_up, lag_down = layer, line - 1 - layer
    lag_out = jnp.maximum(lag_up, lag_down)

    def tick(now):
        @pl.when(now < steps)
        def _():
            beside_copy(now).wait_recv()

        step_up = now - lag_up

        @pl.when(jnp.logical_and(step_up >= 0, step_up < steps))
        def _():
            @pl.when(has_below)
            def _():
                up_copy(step_up).wait_recv()

            @pl.when(has_above)
            def _():
                for slot in range(slots):
                    up_out[step_up, slot] = merged(step_up, slot, up_in[step_up, slot])
                up_copy(step_up).start()

        step_down = now - lag_down

        @pl.when(jnp.logical_and(step_down >= 0, step_down < steps))
        def _():
            @pl.when(has_above)
            def _():
                down_copy(step_down).wait_recv()

            @pl.when(has_below)
            def _():
                for slot in range(slots):
                    down_out[step_down, slot] = merged(step_down, slot, down_in[step_down, slot])
                down_copy(step_down).start()

        step_out = now - lag_out

        @pl.when(jnp.logical_and(step_out >= 0, step_out < steps))
        def _():
            rows = pl.ds(side * half + step_out * CHUNK, CHUNK)
            for slot in range(slots):
                passing = jnp.where(lower[slot], up_in[step_out, slot], down_in[step_out, slot])
                out_ref[slot, rows] = merged(step_out, slot, passing)
            out_copy(step_out, side).start()

    @pl.when(jnp.logical_not(has_below))
    def _():
        up_in[...] = jnp.zeros_like(up_in)

    @pl.when(jnp.logical_not(has_above))
    def _():
        down_in[...] = jnp.zeros_like(down_in)

    each(steps + line - 1, tick)

    def finish(step):
        beside_copy(step).wait_send()

        @pl.when(has_above)
        def _():
            up_copy(step).wait_send()

        @pl.when(has_below)
        def _():
            down_copy(step).wait_send()

        out_copy(step, side).wait_send()
        out_copy(step, 1 - side).wait_recv()

    each(steps, finish)


def spread(owners, blocks, line):
    slots = owners.shape[0]
    count, rows, width = blocks.shape
    steps = count // 2 // CHUNK
    store = pltpu.VMEM((steps, slots, CHUNK, rows, width), blocks.dtype)
    dma = pltpu.SemaphoreType.DMA((steps,))
    return pl.pallas_call(
        functools.partial(spread_kernel, line, slots),
        out_shape=jax.ShapeDtypeStruct((slots, count, rows, width), blocks.dtype),
        in_specs=[
            pl.BlockSpec(memory_space=pltpu.SMEM),
            pl.BlockSpec(memory_space=pltpu.VMEM),
        ],
        out_specs=pl.BlockSpec(memory_space=pltpu.VMEM),
        scratch_shapes=[
            pltpu.VMEM((steps, CHUNK, rows, width), blocks.dtype), store, store, store, store,
        ] + [dma] * 8,
        compiler_params=pltpu.CompilerParams(
            collective_id=0, has_side_effects=True, vmem_limit_bytes=VMEM_LIMIT
        ),
    )(owners, blocks)


def curve_kernel(slots, coef_ref, mine_ref, query_ref, out_ref, shifted, total):
    step = pl.program_id(0)
    channels, rows, width = mine_ref.shape[-3:]
    events = rows // PAIR

    @pl.when(step == 0)
    def _():
        total[...] = jnp.zeros_like(total)

    queries = jnp.concatenate(
        [
            jnp.concatenate(
                [query_ref[slot, side, 0, channel] for side in range(2) for slot in range(slots)],
                axis=0,
            )
            for channel in range(channels)
        ],
        axis=1,
    )
    columns = queries.shape[0]
    lane = lax.broadcasted_iota(jnp.int32, (events, columns), 1)
    second = (lane // events) % PAIR == 1
    later = lane >= columns // 2
    curves = []
    for side in range(2):
        for channel in range(channels):
            row = mine_ref[side, 0, channel].astype(jnp.float32)
            row = jnp.concatenate([row, jnp.zeros((rows, 128), jnp.float32)], axis=1)
            for index in range(LAGS):
                shift = (index - LAGS // 2) % (width + 128)
                moved = pltpu.roll(row, shift, axis=1) if shift else row
                shifted[side, pl.ds(index * rows, rows), pl.ds(channel * width, width)] = (
                    moved[:, :width].astype(jnp.bfloat16)
                )
        curves.append(
            lax.dot_general(
                shifted[side], queries, (((1,), (1,)), ((), ())),
                preferred_element_type=jnp.float32,
            ).reshape(LAGS, PAIR, events, columns)
        )
    picked = [jnp.where(second[None], each[:, 1], each[:, 0]) for each in curves]
    curve = jnp.where(later[None], picked[1], picked[0])
    for group in range(GROUPS):
        total[group] += curve * coef_ref[0, group][None, None, :]

    @pl.when(step == pl.num_programs(0) - 1)
    def _():
        quarter = LAGS // 4
        place = (lane // (columns // 2)) * 2 + (lane // events) % PAIR
        for group in range(GROUPS):
            values = total[group].reshape(LAGS * events, columns)
            values = values + pltpu.roll(values, columns // 2, axis=1)
            ahead = pltpu.roll(values, columns - events, axis=1)
            behind = pltpu.roll(values, events, axis=1)
            flag = (lax.broadcasted_iota(jnp.int32, values.shape, 1) // events) % PAIR == 1
            values = (values + jnp.where(flag, behind, ahead)).reshape(LAGS, events, columns)
            packed = values[:quarter]
            for part in range(1, 4):
                packed = jnp.where(
                    (place == part)[None], values[part * quarter : (part + 1) * quarter], packed
                )
            out_ref[group] = packed


def curves(coef, mine, queries):
    slots = queries.shape[0]
    channels, rows, width = mine.shape[-3:]
    steps = mine.shape[1]
    events = rows // PAIR
    columns = 2 * slots * rows
    return pl.pallas_call(
        functools.partial(curve_kernel, slots),
        grid=(steps,),
        out_shape=jax.ShapeDtypeStruct((GROUPS, LAGS // 4, events, columns), jnp.float32),
        in_specs=[
            pl.BlockSpec((1, GROUPS, columns), lambda i: (i, 0, 0)),
            pl.BlockSpec((2, 1, channels, rows, width), lambda i: (0, i, 0, 0, 0)),
            pl.BlockSpec((slots, 2, 1, channels, rows, width), lambda i: (0, 0, i, 0, 0, 0)),
        ],
        out_specs=pl.BlockSpec(
            (GROUPS, LAGS // 4, events, columns), lambda i: (0, 0, 0, 0)
        ),
        scratch_shapes=[
            pltpu.VMEM((2, LAGS * rows, channels * width), jnp.bfloat16),
            pltpu.VMEM((GROUPS, LAGS, events, columns), jnp.float32),
        ],
        compiler_params=pltpu.CompilerParams(vmem_limit_bytes=VMEM_LIMIT),
    )(coef, mine, queries)


def peak_kernel(parts, part_ref, out_ref, landed, send, recv, back_send, back_recv):
    tile, sta = lax.axis_index("tile"), lax.axis_index("sta")
    share = GROUPS // parts
    barrier = pltpu.get_barrier_semaphore()
    for hop in range(1, parts):
        pl.semaphore_signal(
            barrier, inc=1, device_id=(tile, lax.rem(sta + hop, parts)), device_id_type=MESH
        )
    pl.semaphore_wait(barrier, parts - 1)
    copies = []
    for hop in range(1, parts):
        target = lax.rem(sta + hop, parts)
        copy = pltpu.make_async_remote_copy(
            src_ref=part_ref.at[pl.ds(target * share, share)], dst_ref=landed.at[hop - 1],
            send_sem=send.at[hop - 1], recv_sem=recv.at[hop - 1],
            device_id=(tile, target), device_id_type=MESH,
        )
        copy.start()
        copies.append(copy)
    total = part_ref[pl.ds(sta * share, share)]
    for hop in range(1, parts):
        copies[hop - 1].wait_recv()
        total = total + landed[hop - 1]
    highest = jnp.max(total, axis=1)
    rows, columns = highest.shape[1:]
    highest = highest.reshape(share * rows, columns)
    highest = jnp.maximum(highest, pltpu.roll(highest, columns // 2, axis=1))
    flag = (lax.broadcasted_iota(jnp.int32, highest.shape, 1) // rows) % PAIR == 1
    highest = jnp.maximum(
        highest,
        jnp.where(
            flag, pltpu.roll(highest, rows, axis=1), pltpu.roll(highest, columns - rows, axis=1)
        ),
    )
    out_ref[pl.ds(sta * share, share)] = highest.reshape(share, rows, columns)
    backs = []
    for hop in range(1, parts):
        mine = pl.ds(sta * share, share)
        copy = pltpu.make_async_remote_copy(
            src_ref=out_ref.at[mine], dst_ref=out_ref.at[mine],
            send_sem=back_send.at[hop - 1], recv_sem=back_recv.at[hop - 1],
            device_id=(tile, lax.rem(sta + hop, parts)), device_id_type=MESH,
        )
        copy.start()
        backs.append(copy)
    for copy in copies:
        copy.wait_send()
    for hop in range(1, parts):
        backs[hop - 1].wait_send()
        theirs = pl.ds(lax.rem(sta + parts - hop, parts) * share, share)
        pltpu.make_async_remote_copy(
            src_ref=out_ref.at[theirs], dst_ref=out_ref.at[theirs],
            send_sem=back_send.at[hop - 1], recv_sem=back_recv.at[hop - 1],
            device_id=(tile, lax.rem(sta + hop, parts)), device_id_type=MESH,
        ).wait_recv()


def peaks(part, parts):
    groups, quarter, events, columns = part.shape
    share = groups // parts
    dma = pltpu.SemaphoreType.DMA((parts - 1,))
    return pl.pallas_call(
        functools.partial(peak_kernel, parts),
        out_shape=jax.ShapeDtypeStruct((groups, events, columns), jnp.float32),
        in_specs=[pl.BlockSpec(memory_space=pltpu.VMEM)],
        out_specs=pl.BlockSpec(memory_space=pltpu.VMEM),
        scratch_shapes=[
            pltpu.VMEM((parts - 1, share, quarter, events, columns), jnp.float32),
            dma, dma, dma, dma,
        ],
        compiler_params=pltpu.CompilerParams(
            collective_id=1, has_side_effects=True, vmem_limit_bytes=VMEM_LIMIT
        ),
    )(part)


def shards(tiles, parts, waves, valid, station_group, owners):
    stations, events, channels, samples = waves.shape
    slots = owners.shape[0]
    flags = jnp.concatenate([valid, station_group[:, None]], axis=1)
    everyone = lax.all_gather(flags, ("tile", "sta")).reshape(tiles, parts * stations, events + 1)

    pairs = stations // PAIR
    normed = normalize(waves, valid).reshape(pairs, PAIR, events, channels, samples)
    normed = normed.transpose(0, 3, 1, 2, 4).reshape(pairs * channels, PAIR * events, samples)
    queries = spread(owners, normed, tiles // 2)

    steps = pairs // 2
    shape = (2, steps, channels, PAIR * events, samples)
    onehot = (station_group[:, None] == jnp.arange(GROUPS, dtype=jnp.int32)[None, :]).astype(
        jnp.float32
    )
    coef = onehot.reshape(2, steps, PAIR, GROUPS).transpose(1, 3, 0, 2)
    coef = jnp.broadcast_to(
        coef[:, :, :, None, :, None], (steps, GROUPS, 2, slots, PAIR, events)
    ).reshape(steps, GROUPS, 2 * slots * PAIR * events)
    part = curves(coef, normed.reshape(shape), queries.reshape((slots,) + shape))
    highest = peaks(part, parts)
    highest = highest.reshape(GROUPS, events, 2, slots, PAIR, events)[:, :, 0, :, 0, :]
    highest = highest.reshape(GROUPS, events, slots * events).transpose(0, 2, 1)

    group_of = everyone[0, :, events]
    whole_onehot = (group_of[:, None] == jnp.arange(GROUPS, dtype=jnp.int32)[None, :]).astype(
        jnp.bfloat16
    )
    flags_of = everyone[:, :, :events].astype(jnp.bfloat16)
    query_valid = jnp.take(flags_of, owners, axis=0).transpose(1, 0, 2).reshape(-1, slots * events)
    local_valid = flags_of[lax.axis_index("tile")]
    common = jnp.einsum(
        "gsq,se->gqe", whole_onehot.T[:, :, None] * query_valid[None], local_valid,
        preferred_element_type=jnp.float32,
    )
    return highest / (samples * jnp.maximum(common, 1.0))


def solution(mesh):
    return jax.shard_map(
        functools.partial(shards, mesh.shape["tile"], mesh.shape["sta"]),
        mesh=mesh,
        in_specs=(P("sta", "tile", None, None), P("sta", "tile"), P("sta"), P()),
        out_specs=P(None, None, "tile"),
        check_vma=False,
    )
```

```python
import functools

import jax
import jax.numpy as jnp
from jax import lax
from jax.experimental import pallas as pl
from jax.experimental.pallas import tpu as pltpu
from jax.sharding import PartitionSpec as P

LAGS = 64
GROUPS = 8
PAIR = 2
CHUNK = 2
epsilon = 1e-06
MESH = pl.DeviceIdType.MESH
VMEM_LIMIT = 56 * 1024 * 1024


def normalize(raw_block, mask_block):
    signal = raw_block.astype(jnp.float32)
    inverse_rms = lax.rsqrt(jnp.mean(signal * signal, axis=-1, keepdims=True) + epsilon)
    return (signal * inverse_rms * mask_block[:, :, None, None].astype(jnp.float32)).astype(
        jnp.bfloat16
    )


def spread_kernel(
    line, slots, owners_ref, mine_ref, flags_ref, out_ref, everyone_ref,
    beside, up_out, up_in, down_out, down_in,
    beside_send, beside_recv, up_send, up_recv, down_send, down_recv, out_send, out_recv,
    flags_send, flags_recv, flags_local,
):
    tile, sta = lax.axis_index("tile"), lax.axis_index("sta")
    layer, side = tile // 2, tile % 2
    other = layer * 2 + (1 - side)
    half = mine_ref.shape[0] // 2
    steps = half // CHUNK
    above, below = layer * 2 + 2 + side, layer * 2 - 2 + side
    has_above, has_below = layer < line - 1, layer > 0

    tiles = 2 * line

    def each(count, body):
        def run(index, carry):
            body(index)
            return carry

        lax.fori_loop(0, count, run, 0)

    barrier = pltpu.get_barrier_semaphore()
    each(
        tiles - 1,
        lambda hop: pl.semaphore_signal(
            barrier, inc=1, device_id=(lax.rem(tile + 1 + hop, tiles), sta), device_id_type=MESH
        ),
    )
    pl.semaphore_wait(barrier, tiles - 1)

    def flags_copy(hop, row):
        return pltpu.make_async_remote_copy(
            src_ref=flags_ref, dst_ref=everyone_ref.at[row],
            send_sem=flags_send.at[hop], recv_sem=flags_recv.at[hop],
            device_id=(lax.rem(tile + 1 + hop, tiles), sta), device_id_type=MESH,
        )

    def beside_copy(step):
        return pltpu.make_async_remote_copy(
            src_ref=mine_ref.at[pl.ds((1 - side) * half + step * CHUNK, CHUNK)],
            dst_ref=beside.at[step],
            send_sem=beside_send.at[step], recv_sem=beside_recv.at[step],
            device_id=(other, sta), device_id_type=MESH,
        )

    def up_copy(step):
        return pltpu.make_async_remote_copy(
            src_ref=up_out.at[step], dst_ref=up_in.at[step],
            send_sem=up_send.at[step], recv_sem=up_recv.at[step],
            device_id=(above, sta), device_id_type=MESH,
        )

    def down_copy(step):
        return pltpu.make_async_remote_copy(
            src_ref=down_out.at[step], dst_ref=down_in.at[step],
            send_sem=down_send.at[step], recv_sem=down_recv.at[step],
            device_id=(below, sta), device_id_type=MESH,
        )

    def out_copy(step, of_side):
        rows = pl.ds(of_side * half + step * CHUNK, CHUNK)
        return pltpu.make_async_remote_copy(
            src_ref=out_ref.at[:, rows], dst_ref=out_ref.at[:, rows],
            send_sem=out_send.at[step], recv_sem=out_recv.at[step],
            device_id=(other, sta), device_id_type=MESH,
        )

    each(steps, lambda step: beside_copy(step).start())
    each(tiles - 1, lambda hop: flags_copy(hop, tile).start())
    own_flags = pltpu.make_async_copy(flags_ref, everyone_ref.at[tile], flags_local)
    own_flags.start()
    own = [owners_ref[slot] == tile for slot in range(slots)]
    near = [owners_ref[slot] == other for slot in range(slots)]
    lower = [owners_ref[slot] < layer * 2 for slot in range(slots)]

    def merged(step, slot, passing):
        local = mine_ref[pl.ds(side * half + step * CHUNK, CHUNK)]
        return jnp.where(own[slot], local, jnp.where(near[slot], beside[step], passing))

    lag_up, lag_down = layer, line - 1 - layer
    lag_out = jnp.maximum(lag_up, lag_down)

    def tick(now):
        @pl.when(now < steps)
        def _():
            beside_copy(now).wait_recv()

        step_up = now - lag_up

        @pl.when(jnp.logical_and(step_up >= 0, step_up < steps))
        def _():
            @pl.when(has_below)
            def _():
                up_copy(step_up).wait_recv()

            @pl.when(has_above)
            def _():
                for slot in range(slots):
                    up_out[step_up, slot] = merged(step_up, slot, up_in[step_up, slot])
                up_copy(step_up).start()

        step_down = now - lag_down

        @pl.when(jnp.logical_and(step_down >= 0, step_down < steps))
        def _():
            @pl.when(has_above)
            def _():
                down_copy(step_down).wait_recv()

            @pl.when(has_below)
            def _():
                for slot in range(slots):
                    down_out[step_down, slot] = merged(step_down, slot, down_in[step_down, slot])
                down_copy(step_down).start()

        step_out = now - lag_out

        @pl.when(jnp.logical_and(step_out >= 0, step_out < steps))
        def _():
            rows = pl.ds(side * half + step_out * CHUNK, CHUNK)
            for slot in range(slots):
                passing = jnp.where(lower[slot], up_in[step_out, slot], down_in[step_out, slot])
                out_ref[slot, rows] = merged(step_out, slot, passing)
            out_copy(step_out, side).start()

    @pl.when(jnp.logical_not(has_below))
    def _():
        up_in[...] = jnp.zeros_like(up_in)

    @pl.when(jnp.logical_not(has_above))
    def _():
        down_in[...] = jnp.zeros_like(down_in)

    each(steps + line - 1, tick)

    def finish(step):
        beside_copy(step).wait_send()

        @pl.when(has_above)
        def _():
            up_copy(step).wait_send()

        @pl.when(has_below)
        def _():
            down_copy(step).wait_send()

        out_copy(step, side).wait_send()
        out_copy(step, 1 - side).wait_recv()

    each(steps, finish)
    own_flags.wait()

    def finish_flags(hop):
        flags_copy(hop, tile).wait_send()
        flags_copy(hop, lax.rem(tile + tiles - 1 - hop, tiles)).wait_recv()

    each(tiles - 1, finish_flags)


def spread(owners, blocks, flags, line):
    slots = owners.shape[0]
    count, rows, width = blocks.shape
    steps = count // 2 // CHUNK
    store = pltpu.VMEM((steps, slots, CHUNK, rows, width), blocks.dtype)
    dma = pltpu.SemaphoreType.DMA((steps,))
    return pl.pallas_call(
        functools.partial(spread_kernel, line, slots),
        out_shape=(
            jax.ShapeDtypeStruct((slots, count, rows, width), blocks.dtype),
            jax.ShapeDtypeStruct((2 * line,) + flags.shape, flags.dtype),
        ),
        in_specs=[
            pl.BlockSpec(memory_space=pltpu.SMEM),
            pl.BlockSpec(memory_space=pltpu.VMEM),
            pl.BlockSpec(memory_space=pltpu.VMEM),
        ],
        out_specs=(
            pl.BlockSpec(memory_space=pltpu.VMEM),
            pl.BlockSpec(memory_space=pltpu.VMEM),
        ),
        scratch_shapes=[
            pltpu.VMEM((steps, CHUNK, rows, width), blocks.dtype), store, store, store, store,
        ] + [dma] * 8 + [
            pltpu.SemaphoreType.DMA((2 * line - 1,)), pltpu.SemaphoreType.DMA((2 * line - 1,)),
            pltpu.SemaphoreType.DMA,
        ],
        compiler_params=pltpu.CompilerParams(
            collective_id=0, has_side_effects=True, vmem_limit_bytes=VMEM_LIMIT
        ),
    )(owners, blocks, flags)


def curve_kernel(
    slots, owners_ref, coef_ref, member_ref, everyone_ref, mine_ref, query_ref,
    out_ref, common_ref, shifted, total,
):
    step = pl.program_id(0)
    channels, rows, width = mine_ref.shape[-3:]
    events = rows // PAIR

    @pl.when(step == 0)
    def _():
        total[...] = jnp.zeros_like(total)

    queries = jnp.concatenate(
        [
            jnp.concatenate(
                [query_ref[slot, side, 0, channel] for side in range(2) for slot in range(slots)],
                axis=0,
            )
            for channel in range(channels)
        ],
        axis=1,
    )
    columns = queries.shape[0]
    lane = lax.broadcasted_iota(jnp.int32, (events, columns), 1)
    second = (lane // events) % PAIR == 1
    later = lane >= columns // 2
    curves = []
    for side in range(2):
        for channel in range(channels):
            row = mine_ref[side, 0, channel].astype(jnp.float32)
            row = jnp.concatenate([row, jnp.zeros((rows, 128), jnp.float32)], axis=1)
            for index in range(LAGS):
                shift = (index - LAGS // 2) % (width + 128)
                moved = pltpu.roll(row, shift, axis=1) if shift else row
                shifted[side, pl.ds(index * rows, rows), pl.ds(channel * width, width)] = (
                    moved[:, :width].astype(jnp.bfloat16)
                )
        curves.append(
            lax.dot_general(
                shifted[side], queries, (((1,), (1,)), ((), ())),
                preferred_element_type=jnp.float32,
            ).reshape(LAGS, PAIR, events, columns)
        )
    picked = [jnp.where(second[None], each[:, 1], each[:, 0]) for each in curves]
    curve = jnp.where(later[None], picked[1], picked[0])
    for group in range(GROUPS):
        total[group] += curve * coef_ref[0, group][None, None, :]

    @pl.when(step == pl.num_programs(0) - 1)
    def _():
        quarter = LAGS // 4
        place = (lane // (columns // 2)) * 2 + (lane // events) % PAIR
        for group in range(GROUPS):
            values = total[group].reshape(LAGS * events, columns)
            values = values + pltpu.roll(values, columns // 2, axis=1)
            ahead = pltpu.roll(values, columns - events, axis=1)
            behind = pltpu.roll(values, events, axis=1)
            flag = (lax.broadcasted_iota(jnp.int32, values.shape, 1) // events) % PAIR == 1
            values = (values + jnp.where(flag, behind, ahead)).reshape(LAGS, events, columns)
            packed = values[:quarter]
            for part in range(1, 4):
                packed = jnp.where(
                    (place == part)[None], values[part * quarter : (part + 1) * quarter], packed
                )
            out_ref[group] = packed
        flags = [everyone_ref[owners_ref[slot]] for slot in range(slots)]
        flags = jnp.concatenate([each for each in flags for _ in range(PAIR)] * 2, axis=0)
        common_ref[...] = lax.dot_general(
            member_ref[...], flags, (((1,), (1,)), ((), ())), preferred_element_type=jnp.float32
        ).reshape(common_ref.shape)


def curves(owners, coef, member, everyone, mine, queries):
    slots = queries.shape[0]
    channels, rows, width = mine.shape[-3:]
    steps = mine.shape[1]
    events = rows // PAIR
    columns = 2 * slots * rows
    return pl.pallas_call(
        functools.partial(curve_kernel, slots),
        grid=(steps,),
        out_shape=(
            jax.ShapeDtypeStruct((GROUPS, LAGS // 4, events, columns), jnp.float32),
            jax.ShapeDtypeStruct((GROUPS, events, columns), jnp.float32),
        ),
        in_specs=[
            pl.BlockSpec(memory_space=pltpu.SMEM),
            pl.BlockSpec((1, GROUPS, columns), lambda i: (i, 0, 0)),
            pl.BlockSpec(memory_space=pltpu.VMEM),
            pl.BlockSpec(memory_space=pltpu.VMEM),
            pl.BlockSpec((2, 1, channels, rows, width), lambda i: (0, i, 0, 0, 0)),
            pl.BlockSpec((slots, 2, 1, channels, rows, width), lambda i: (0, 0, i, 0, 0, 0)),
        ],
        out_specs=(
            pl.BlockSpec((GROUPS, LAGS // 4, events, columns), lambda i: (0, 0, 0, 0)),
            pl.BlockSpec((GROUPS, events, columns), lambda i: (0, 0, 0)),
        ),
        scratch_shapes=[
            pltpu.VMEM((2, LAGS * rows, channels * width), jnp.bfloat16),
            pltpu.VMEM((GROUPS, LAGS, events, columns), jnp.float32),
        ],
        compiler_params=pltpu.CompilerParams(vmem_limit_bytes=VMEM_LIMIT),
    )(owners, coef, member, everyone, mine, queries)


def peak_kernel(
    parts, samples, part_ref, common_ref, out_ref, landed, counted,
    send, recv, count_send, count_recv, back_send, back_recv,
):
    tile, sta = lax.axis_index("tile"), lax.axis_index("sta")
    share = GROUPS // parts
    barrier = pltpu.get_barrier_semaphore()
    for hop in range(1, parts):
        pl.semaphore_signal(
            barrier, inc=1, device_id=(tile, lax.rem(sta + hop, parts)), device_id_type=MESH
        )
    pl.semaphore_wait(barrier, parts - 1)
    copies = []
    for hop in range(1, parts):
        target = lax.rem(sta + hop, parts)
        copy = pltpu.make_async_remote_copy(
            src_ref=part_ref.at[pl.ds(target * share, share)], dst_ref=landed.at[hop - 1],
            send_sem=send.at[hop - 1], recv_sem=recv.at[hop - 1],
            device_id=(tile, target), device_id_type=MESH,
        )
        copy.start()
        copies.append(copy)
    counts = []
    for hop in range(1, parts):
        target = lax.rem(sta + hop, parts)
        copy = pltpu.make_async_remote_copy(
            src_ref=common_ref.at[pl.ds(target * share, share)], dst_ref=counted.at[hop - 1],
            send_sem=count_send.at[hop - 1], recv_sem=count_recv.at[hop - 1],
            device_id=(tile, target), device_id_type=MESH,
        )
        copy.start()
        counts.append(copy)
    common = common_ref[pl.ds(sta * share, share)]
    total = part_ref[pl.ds(sta * share, share)]
    for hop in range(1, parts):
        copies[hop - 1].wait_recv()
        total = total + landed[hop - 1]
    for hop in range(1, parts):
        counts[hop - 1].wait_recv()
        common = common + counted[hop - 1]
    highest = jnp.max(total, axis=1)
    rows, columns = highest.shape[1:]
    highest = highest.reshape(share * rows, columns)
    highest = jnp.maximum(highest, pltpu.roll(highest, columns // 2, axis=1))
    flag = (lax.broadcasted_iota(jnp.int32, highest.shape, 1) // rows) % PAIR == 1
    highest = jnp.maximum(
        highest,
        jnp.where(
            flag, pltpu.roll(highest, rows, axis=1), pltpu.roll(highest, columns - rows, axis=1)
        ),
    )
    out_ref[pl.ds(sta * share, share)] = highest.reshape(share, rows, columns) / (
        samples * jnp.maximum(common, 1.0)
    )
    backs = []
    for hop in range(1, parts):
        mine = pl.ds(sta * share, share)
        copy = pltpu.make_async_remote_copy(
            src_ref=out_ref.at[mine], dst_ref=out_ref.at[mine],
            send_sem=back_send.at[hop - 1], recv_sem=back_recv.at[hop - 1],
            device_id=(tile, lax.rem(sta + hop, parts)), device_id_type=MESH,
        )
        copy.start()
        backs.append(copy)
    for copy in copies + counts:
        copy.wait_send()
    for hop in range(1, parts):
        backs[hop - 1].wait_send()
        theirs = pl.ds(lax.rem(sta + parts - hop, parts) * share, share)
        pltpu.make_async_remote_copy(
            src_ref=out_ref.at[theirs], dst_ref=out_ref.at[theirs],
            send_sem=back_send.at[hop - 1], recv_sem=back_recv.at[hop - 1],
            device_id=(tile, lax.rem(sta + hop, parts)), device_id_type=MESH,
        ).wait_recv()


def peaks(part, common, samples, parts):
    groups, quarter, events, columns = part.shape
    share = groups // parts
    dma = pltpu.SemaphoreType.DMA((parts - 1,))
    return pl.pallas_call(
        functools.partial(peak_kernel, parts, float(samples)),
        out_shape=jax.ShapeDtypeStruct((groups, events, columns), jnp.float32),
        in_specs=[pl.BlockSpec(memory_space=pltpu.VMEM)] * 2,
        out_specs=pl.BlockSpec(memory_space=pltpu.VMEM),
        scratch_shapes=[
            pltpu.VMEM((parts - 1, share, quarter, events, columns), jnp.float32),
            pltpu.VMEM((parts - 1, share, events, columns), jnp.float32),
            dma, dma, dma, dma, dma, dma,
        ],
        compiler_params=pltpu.CompilerParams(
            collective_id=1, has_side_effects=True, vmem_limit_bytes=VMEM_LIMIT
        ),
    )(part, common)


def shards(tiles, parts, waves, valid, station_group, owners):
    stations, events, channels, samples = waves.shape
    slots = owners.shape[0]
    flags = jnp.pad(valid.T.astype(jnp.float32), ((0, 0), (0, -stations % 128)))

    pairs = stations // PAIR
    normed = normalize(waves, valid).reshape(pairs, PAIR, events, channels, samples)
    normed = normed.transpose(0, 3, 1, 2, 4).reshape(pairs * channels, PAIR * events, samples)
    queries, everyone = spread(owners, normed, flags, tiles // 2)

    steps = pairs // 2
    shape = (2, steps, channels, PAIR * events, samples)
    onehot = (station_group[:, None] == jnp.arange(GROUPS, dtype=jnp.int32)[None, :]).astype(
        jnp.float32
    )
    coef = onehot.reshape(2, steps, PAIR, GROUPS).transpose(1, 3, 0, 2)
    coef = jnp.broadcast_to(
        coef[:, :, :, None, :, None], (steps, GROUPS, 2, slots, PAIR, events)
    ).reshape(steps, GROUPS, 2 * slots * PAIR * events)
    members = jnp.pad(onehot.T, ((0, 0), (0, -stations % 128)))
    member = (members[:, None, :] * flags[None]).reshape(GROUPS * events, -1)
    part, common = curves(
        owners, coef, member, everyone, normed.reshape(shape), queries.reshape((slots,) + shape)
    )
    highest = peaks(part, common, samples, parts)
    highest = highest.reshape(GROUPS, events, 2, slots, PAIR, events)[:, :, 0, :, 0, :]
    return highest.reshape(GROUPS, events, slots * events).transpose(0, 2, 1)


def solution(mesh):
    return jax.shard_map(
        functools.partial(shards, mesh.shape["tile"], mesh.shape["sta"]),
        mesh=mesh,
        in_specs=(P("sta", "tile", None, None), P("sta", "tile"), P("sta"), P()),
        out_specs=P(None, None, "tile"),
        check_vma=False,
    )
```

```python
import functools

import jax
import jax.numpy as jnp
from jax import lax
from jax.experimental import pallas as pl
from jax.experimental.pallas import tpu as pltpu
from jax.sharding import PartitionSpec as P

LAGS = 64
GROUPS = 8
PAIR = 2
CHUNK = 1
HOP = 2
AHEAD = 4
epsilon = 1e-06
MESH = pl.DeviceIdType.MESH
VMEM_LIMIT = 56 * 1024 * 1024


def normalize(raw_block, mask_block):
    signal = raw_block.astype(jnp.float32)
    inverse_rms = lax.rsqrt(jnp.mean(signal * signal, axis=-1, keepdims=True) + epsilon)
    return (signal * inverse_rms * mask_block[:, :, None, None].astype(jnp.float32)).astype(
        jnp.bfloat16
    )


def peak_kernel(
    line, parts, slots, samples,
    owners_ref, mine_ref, flags_ref, coef_ref, member_ref, peak_ref,
    out_ref, everyone_ref, shifted, products, total, part, landed, common_ref, counted,
    beside, up_out, up_in, down_out, down_in,
    beside_send, beside_recv, up_send, up_recv, down_send, down_recv, out_send, out_recv,
    flags_send, flags_recv, flags_local,
    send, recv, count_send, count_recv, back_send, back_recv,
):
    tile, sta = lax.axis_index("tile"), lax.axis_index("sta")
    layer, side = tile // 2, tile % 2
    other = layer * 2 + (1 - side)
    half = mine_ref.shape[0] // 2
    steps = half // CHUNK
    above, below = layer * 2 + 2 + side, layer * 2 - 2 + side
    has_above, has_below = layer < line - 1, layer > 0

    tiles = 2 * line

    def each(count, body):
        def run(index, carry):
            body(index)
            return carry

        lax.fori_loop(0, count, run, 0)

    barrier = pltpu.get_barrier_semaphore()
    each(
        tiles - 1,
        lambda hop: pl.semaphore_signal(
            barrier, inc=1, device_id=(lax.rem(tile + 1 + hop, tiles), sta), device_id_type=MESH
        ),
    )
    for hop in range(1, parts):
        pl.semaphore_signal(
            barrier, inc=1, device_id=(tile, lax.rem(sta + hop, parts)), device_id_type=MESH
        )
    pl.semaphore_wait(barrier, tiles - 1 + parts - 1)

    def flags_copy(hop, row):
        return pltpu.make_async_remote_copy(
            src_ref=flags_ref, dst_ref=everyone_ref.at[row],
            send_sem=flags_send.at[hop], recv_sem=flags_recv.at[hop],
            device_id=(lax.rem(tile + 1 + hop, tiles), sta), device_id_type=MESH,
        )

    def beside_copy(step):
        return pltpu.make_async_remote_copy(
            src_ref=mine_ref.at[pl.ds((1 - side) * half + step * CHUNK, CHUNK)],
            dst_ref=beside.at[step],
            send_sem=beside_send.at[step], recv_sem=beside_recv.at[step],
            device_id=(other, sta), device_id_type=MESH,
        )

    def up_copy(step):
        return pltpu.make_async_remote_copy(
            src_ref=up_out.at[step], dst_ref=up_in.at[step],
            send_sem=up_send.at[step], recv_sem=up_recv.at[step],
            device_id=(above, sta), device_id_type=MESH,
        )

    def down_copy(step):
        return pltpu.make_async_remote_copy(
            src_ref=down_out.at[step], dst_ref=down_in.at[step],
            send_sem=down_send.at[step], recv_sem=down_recv.at[step],
            device_id=(below, sta), device_id_type=MESH,
        )

    def out_copy(step, of_side):
        rows = pl.ds(of_side * half + step * CHUNK, CHUNK)
        return pltpu.make_async_remote_copy(
            src_ref=out_ref.at[:, rows], dst_ref=out_ref.at[:, rows],
            send_sem=out_send.at[step], recv_sem=out_recv.at[step],
            device_id=(other, sta), device_id_type=MESH,
        )

    each(AHEAD, lambda step: beside_copy(step).start())
    each(tiles - 1, lambda hop: flags_copy(hop, tile).start())
    own_flags = pltpu.make_async_copy(flags_ref, everyone_ref.at[tile], flags_local)
    own_flags.start()
    own = [owners_ref[slot] == tile for slot in range(slots)]
    near = [owners_ref[slot] == other for slot in range(slots)]
    lower = [owners_ref[slot] < layer * 2 for slot in range(slots)]

    def merged(step, slot, passing):
        local = mine_ref[pl.ds(side * half + step * CHUNK, CHUNK)]
        return jnp.where(own[slot], local, jnp.where(near[slot], beside[step], passing))

    rows, width = mine_ref.shape[-2:]
    events = rows // PAIR
    columns = 2 * slots * rows
    share = GROUPS // parts
    lane = lax.broadcasted_iota(jnp.int32, (events, columns), 1)
    second = (lane // events) % PAIR == 1
    later = lane >= columns // 2
    channels = mine_ref.shape[0] // (2 * coef_ref.shape[0])
    total[...] = jnp.zeros_like(total)

    def correlate(step):
        channel, quad = lax.rem(step, channels), step // channels
        queries = jnp.concatenate(
            [out_ref[slot, of_side * half + step] for of_side in range(2) for slot in range(slots)],
            axis=0,
        )
        for of_side in range(2):
            row = mine_ref[of_side * half + step].astype(jnp.float32)
            row = jnp.concatenate([row, jnp.zeros((rows, 128), jnp.float32)], axis=1)
            for index in range(LAGS):
                shift = (index - LAGS // 2) % (width + 128)
                moved = pltpu.roll(row, shift, axis=1) if shift else row
                shifted[of_side, pl.ds(index * rows, rows)] = moved[:, :width].astype(jnp.bfloat16)
            product = lax.dot_general(
                shifted[of_side], queries, (((1,), (1,)), ((), ())),
                preferred_element_type=jnp.float32,
            )

            @pl.when(channel == 0)
            def _():
                products[of_side] = product

            @pl.when(channel > 0)
            def _():
                products[of_side] += product

        @pl.when(channel == channels - 1)
        def _():
            def gather(index, carry):
                both = [
                    products[of_side, pl.ds(pl.multiple_of(index * rows, rows), rows)]
                    for of_side in range(2)
                ]
                picked = [jnp.where(second, one[events:], one[:events]) for one in both]
                curve = jnp.where(later, picked[1], picked[0])
                for group in range(GROUPS):
                    total[group, index] += curve * coef_ref[quad, pl.ds(group, 1)]
                return carry

            lax.fori_loop(0, LAGS, gather, 0, unroll=4)

    lag_up, lag_down = HOP * layer, HOP * (line - 1 - layer)
    lag_out = jnp.maximum(lag_up, lag_down)

    def tick(now):
        @pl.when(now < steps)
        def _():
            beside_copy(now).wait_recv()

        @pl.when(now + AHEAD < steps)
        def _():
            beside_copy(now + AHEAD).start()

        step_up = now - lag_up

        @pl.when(jnp.logical_and(step_up >= 0, step_up < steps))
        def _():
            @pl.when(has_below)
            def _():
                up_copy(step_up).wait_recv()

            @pl.when(has_above)
            def _():
                for slot in range(slots):
                    up_out[step_up, slot] = merged(step_up, slot, up_in[step_up, slot])
                up_copy(step_up).start()

        step_down = now - lag_down

        @pl.when(jnp.logical_and(step_down >= 0, step_down < steps))
        def _():
            @pl.when(has_above)
            def _():
                down_copy(step_down).wait_recv()

            @pl.when(has_below)
            def _():
                for slot in range(slots):
                    down_out[step_down, slot] = merged(step_down, slot, down_in[step_down, slot])
                down_copy(step_down).start()

        step_out = now - lag_out

        @pl.when(jnp.logical_and(step_out >= 0, step_out < steps))
        def _():
            rows = pl.ds(side * half + step_out * CHUNK, CHUNK)
            for slot in range(slots):
                passing = jnp.where(lower[slot], up_in[step_out, slot], down_in[step_out, slot])
                out_ref[slot, rows] = merged(step_out, slot, passing)
            out_copy(step_out, side).start()

        step_curve = step_out - HOP

        @pl.when(jnp.logical_and(step_curve >= 0, step_curve < steps))
        def _():
            out_copy(step_curve, 1 - side).wait_recv()
            correlate(step_curve)

    @pl.when(jnp.logical_not(has_below))
    def _():
        up_in[...] = jnp.zeros_like(up_in)

    @pl.when(jnp.logical_not(has_above))
    def _():
        down_in[...] = jnp.zeros_like(down_in)

    each(steps + HOP * line, tick)

    def finish(step):
        beside_copy(step).wait_send()

        @pl.when(has_above)
        def _():
            up_copy(step).wait_send()

        @pl.when(has_below)
        def _():
            down_copy(step).wait_send()

        out_copy(step, side).wait_send()

    each(steps, finish)
    own_flags.wait()

    def finish_flags(hop):
        flags_copy(hop, tile).wait_send()
        flags_copy(hop, lax.rem(tile + tiles - 1 - hop, tiles)).wait_recv()

    each(tiles - 1, finish_flags)

    quarter = LAGS // 4
    place = (lane // (columns // 2)) * 2 + (lane // events) % PAIR
    flags = [everyone_ref[owners_ref[slot]] for slot in range(slots)]
    flags = jnp.concatenate([one for one in flags for _ in range(PAIR)] * 2, axis=0)
    common_ref[...] = lax.dot_general(
        member_ref[...], flags, (((1,), (1,)), ((), ())), preferred_element_type=jnp.float32
    ).reshape(common_ref.shape)

    def pack(group):
        values = total[group].reshape(LAGS * events, columns)
        values = values + pltpu.roll(values, columns // 2, axis=1)
        ahead = pltpu.roll(values, columns - events, axis=1)
        behind = pltpu.roll(values, events, axis=1)
        flag = (lax.broadcasted_iota(jnp.int32, values.shape, 1) // events) % PAIR == 1
        values = (values + jnp.where(flag, behind, ahead)).reshape(LAGS, events, columns)
        packed = values[:quarter]
        for number in range(1, 4):
            packed = jnp.where(
                (place == number)[None], values[number * quarter : (number + 1) * quarter], packed
            )
        part[group] = packed

    copies, counts = [], []
    for hop in range(1, parts + 1):
        target = lax.rem(sta + hop, parts)
        for number in range(share):
            pack(target * share + number)
        if hop == parts:
            break
        theirs = pl.ds(target * share, share)
        for source, place_in, done, came, started in (
            (part, landed, send, recv, copies),
            (common_ref, counted, count_send, count_recv, counts),
        ):
            copy = pltpu.make_async_remote_copy(
                src_ref=source.at[theirs], dst_ref=place_in.at[hop - 1],
                send_sem=done.at[hop - 1], recv_sem=came.at[hop - 1],
                device_id=(tile, target), device_id_type=MESH,
            )
            copy.start()
            started.append(copy)
    ours = pl.ds(sta * share, share)
    common, summed = common_ref[ours], part[ours]
    for hop in range(1, parts):
        copies[hop - 1].wait_recv()
        summed = summed + landed[hop - 1]
    for hop in range(1, parts):
        counts[hop - 1].wait_recv()
        common = common + counted[hop - 1]
    highest = jnp.max(summed, axis=1)
    highest = highest.reshape(share * events, columns)
    highest = jnp.maximum(highest, pltpu.roll(highest, columns // 2, axis=1))
    flag = (lax.broadcasted_iota(jnp.int32, highest.shape, 1) // events) % PAIR == 1
    highest = jnp.maximum(
        highest,
        jnp.where(
            flag, pltpu.roll(highest, events, axis=1), pltpu.roll(highest, columns - events, axis=1)
        ),
    )
    peak_ref[pl.ds(sta * share, share)] = highest.reshape(share, events, columns) / (
        samples * jnp.maximum(common, 1.0)
    )
    backs = []
    for hop in range(1, parts):
        mine = pl.ds(sta * share, share)
        copy = pltpu.make_async_remote_copy(
            src_ref=peak_ref.at[mine], dst_ref=peak_ref.at[mine],
            send_sem=back_send.at[hop - 1], recv_sem=back_recv.at[hop - 1],
            device_id=(tile, lax.rem(sta + hop, parts)), device_id_type=MESH,
        )
        copy.start()
        backs.append(copy)
    for copy in copies + counts:
        copy.wait_send()
    for hop in range(1, parts):
        backs[hop - 1].wait_send()
        theirs = pl.ds(lax.rem(sta + parts - hop, parts) * share, share)
        pltpu.make_async_remote_copy(
            src_ref=peak_ref.at[theirs], dst_ref=peak_ref.at[theirs],
            send_sem=back_send.at[hop - 1], recv_sem=back_recv.at[hop - 1],
            device_id=(tile, lax.rem(sta + hop, parts)), device_id_type=MESH,
        ).wait_recv()


def peaks(owners, blocks, flags, coef, member, line, parts, samples):
    slots = owners.shape[0]
    count, rows, width = blocks.shape
    events = rows // PAIR
    columns = 2 * slots * rows
    share = GROUPS // parts
    steps = count // 2 // CHUNK
    store = pltpu.VMEM((steps, slots, CHUNK, rows, width), blocks.dtype)
    dma = pltpu.SemaphoreType.DMA((steps,))
    dma_tile = pltpu.SemaphoreType.DMA((2 * line - 1,))
    dma_sta = pltpu.SemaphoreType.DMA((parts - 1,))
    return pl.pallas_call(
        functools.partial(peak_kernel, line, parts, slots, float(samples)),
        out_shape=jax.ShapeDtypeStruct((GROUPS, events, columns), jnp.float32),
        in_specs=[pl.BlockSpec(memory_space=pltpu.SMEM)]
        + [pl.BlockSpec(memory_space=pltpu.VMEM)] * 4,
        out_specs=pl.BlockSpec(memory_space=pltpu.VMEM),
        scratch_shapes=[
            pltpu.VMEM((slots, count, rows, width), blocks.dtype),
            pltpu.VMEM((2 * line,) + flags.shape, flags.dtype),
            pltpu.VMEM((2, LAGS * rows, width), blocks.dtype),
            pltpu.VMEM((2, LAGS * rows, columns), jnp.float32),
            pltpu.VMEM((GROUPS, LAGS, events, columns), jnp.float32),
            pltpu.VMEM((GROUPS, LAGS // 4, events, columns), jnp.float32),
            pltpu.VMEM((parts - 1, share, LAGS // 4, events, columns), jnp.float32),
            pltpu.VMEM((GROUPS, events, columns), jnp.float32),
            pltpu.VMEM((parts - 1, share, events, columns), jnp.float32),
            pltpu.VMEM((steps, CHUNK, rows, width), blocks.dtype), store, store, store, store,
        ]
        + [dma] * 8
        + [dma_tile, dma_tile, pltpu.SemaphoreType.DMA]
        + [dma_sta] * 6,
        compiler_params=pltpu.CompilerParams(
            collective_id=0, has_side_effects=True, vmem_limit_bytes=VMEM_LIMIT
        ),
    )(owners, blocks, flags, coef, member)


def shards(tiles, parts, waves, valid, station_group, owners):
    stations, events, channels, samples = waves.shape
    slots = owners.shape[0]
    flags = jnp.pad(valid.T.astype(jnp.float32), ((0, 0), (0, -stations % 128)))

    pairs = stations // PAIR
    normed = normalize(waves, valid).reshape(pairs, PAIR, events, channels, samples)
    normed = normed.transpose(0, 3, 1, 2, 4).reshape(pairs * channels, PAIR * events, samples)

    steps = pairs // 2
    onehot = (station_group[:, None] == jnp.arange(GROUPS, dtype=jnp.int32)[None, :]).astype(
        jnp.float32
    )
    coef = onehot.reshape(2, steps, PAIR, GROUPS).transpose(1, 3, 0, 2)
    coef = jnp.broadcast_to(
        coef[:, :, :, None, :, None], (steps, GROUPS, 2, slots, PAIR, events)
    ).reshape(steps, GROUPS, 2 * slots * PAIR * events)
    members = jnp.pad(onehot.T, ((0, 0), (0, -stations % 128)))
    member = (members[:, None, :] * flags[None]).reshape(GROUPS * events, -1)
    highest = peaks(owners, normed, flags, coef, member, tiles // 2, parts, samples)
    highest = highest.reshape(GROUPS, events, 2, slots, PAIR, events)[:, :, 0, :, 0, :]
    return highest.reshape(GROUPS, events, slots * events).transpose(0, 2, 1)


def solution(mesh):
    return jax.shard_map(
        functools.partial(shards, mesh.shape["tile"], mesh.shape["sta"]),
        mesh=mesh,
        in_specs=(P("sta", "tile", None, None), P("sta", "tile"), P("sta"), P()),
        out_specs=P(None, None, "tile"),
        check_vma=False,
    )
```

```python
import functools

import jax
import jax.numpy as jnp
from jax import lax
from jax.experimental import pallas as pl
from jax.experimental.pallas import tpu as pltpu
from jax.sharding import PartitionSpec as P

LAGS = 64
GROUPS = 8
PAIR = 2
CHUNK = 1
HOP = 3
AHEAD = 4
epsilon = 1e-06
MESH = pl.DeviceIdType.MESH
VMEM_LIMIT = 56 * 1024 * 1024


def normalize(raw_block, mask_block):
    signal = raw_block.astype(jnp.float32)
    inverse_rms = lax.rsqrt(jnp.mean(signal * signal, axis=-1, keepdims=True) + epsilon)
    return (signal * inverse_rms * mask_block[:, :, None, None].astype(jnp.float32)).astype(
        jnp.bfloat16
    )


def peak_kernel(
    line, parts, slots, samples,
    owners_ref, group_ref, mine_ref, flags_ref, member_ref, peak_ref,
    out_ref, everyone_ref, shifted, products, total, part, landed, common_ref, counted,
    beside, up_out, up_in, down_out, down_in,
    beside_send, beside_recv, up_send, up_recv, down_send, down_recv, out_send, out_recv,
    flags_send, flags_recv, flags_local,
    send, recv, count_send, count_recv, back_send, back_recv,
):
    tile, sta = lax.axis_index("tile"), lax.axis_index("sta")
    layer, side = tile // 2, tile % 2
    other = layer * 2 + (1 - side)
    half = mine_ref.shape[0] // 2
    steps = half // CHUNK
    above, below = layer * 2 + 2 + side, layer * 2 - 2 + side
    has_above, has_below = layer < line - 1, layer > 0

    tiles = 2 * line

    def each(count, body):
        def run(index, carry):
            body(index)
            return carry

        lax.fori_loop(0, count, run, 0)

    barrier = pltpu.get_barrier_semaphore()
    each(
        tiles - 1,
        lambda hop: pl.semaphore_signal(
            barrier, inc=1, device_id=(lax.rem(tile + 1 + hop, tiles), sta), device_id_type=MESH
        ),
    )
    for hop in range(1, parts):
        pl.semaphore_signal(
            barrier, inc=1, device_id=(tile, lax.rem(sta + hop, parts)), device_id_type=MESH
        )
    pl.semaphore_wait(barrier, tiles - 1 + parts - 1)

    def flags_copy(hop, row):
        return pltpu.make_async_remote_copy(
            src_ref=flags_ref, dst_ref=everyone_ref.at[row],
            send_sem=flags_send.at[hop], recv_sem=flags_recv.at[hop],
            device_id=(lax.rem(tile + 1 + hop, tiles), sta), device_id_type=MESH,
        )

    def beside_copy(step):
        return pltpu.make_async_remote_copy(
            src_ref=mine_ref.at[pl.ds((1 - side) * half + step * CHUNK, CHUNK)],
            dst_ref=beside.at[step],
            send_sem=beside_send.at[step], recv_sem=beside_recv.at[step],
            device_id=(other, sta), device_id_type=MESH,
        )

    def up_copy(step):
        return pltpu.make_async_remote_copy(
            src_ref=up_out.at[step], dst_ref=up_in.at[step],
            send_sem=up_send.at[step], recv_sem=up_recv.at[step],
            device_id=(above, sta), device_id_type=MESH,
        )

    def down_copy(step):
        return pltpu.make_async_remote_copy(
            src_ref=down_out.at[step], dst_ref=down_in.at[step],
            send_sem=down_send.at[step], recv_sem=down_recv.at[step],
            device_id=(below, sta), device_id_type=MESH,
        )

    def out_copy(step, of_side):
        rows = pl.ds(of_side * half + step * CHUNK, CHUNK)
        return pltpu.make_async_remote_copy(
            src_ref=out_ref.at[:, rows], dst_ref=out_ref.at[:, rows],
            send_sem=out_send.at[step], recv_sem=out_recv.at[step],
            device_id=(other, sta), device_id_type=MESH,
        )

    each(AHEAD, lambda step: beside_copy(step).start())
    each(tiles - 1, lambda hop: flags_copy(hop, tile).start())
    own_flags = pltpu.make_async_copy(flags_ref, everyone_ref.at[tile], flags_local)
    own_flags.start()
    own = [owners_ref[slot] == tile for slot in range(slots)]
    near = [owners_ref[slot] == other for slot in range(slots)]
    lower = [owners_ref[slot] < layer * 2 for slot in range(slots)]

    def merged(step, slot, passing):
        local = mine_ref[pl.ds(side * half + step * CHUNK, CHUNK)]
        return jnp.where(own[slot], local, jnp.where(near[slot], beside[step], passing))

    rows, width = mine_ref.shape[-2:]
    events = rows // PAIR
    columns = 2 * slots * rows
    share = GROUPS // parts
    lane = lax.broadcasted_iota(jnp.int32, (events, columns), 1)
    second = (lane // events) % PAIR == 1
    later = lane >= columns // 2
    channels = 2 * half // (group_ref.shape[0] // PAIR)
    total[...] = jnp.zeros_like(total)

    def correlate(step):
        channel, quad = lax.rem(step, channels), step // channels
        queries = jnp.concatenate(
            [out_ref[slot, of_side * half + step] for of_side in range(2) for slot in range(slots)],
            axis=0,
        )
        for of_side in range(2):
            row = mine_ref[of_side * half + step].astype(jnp.float32)
            row = jnp.concatenate([row, jnp.zeros((rows, 128), jnp.float32)], axis=1)
            for index in range(LAGS):
                shift = (index - LAGS // 2) % (width + 128)
                moved = pltpu.roll(row, shift, axis=1) if shift else row
                shifted[of_side, pl.ds(index * rows, rows)] = moved[:, :width].astype(jnp.bfloat16)
            product = lax.dot_general(
                shifted[of_side], queries, (((1,), (1,)), ((), ())),
                preferred_element_type=jnp.float32,
            )

            @pl.when(channel == 0)
            def _():
                products[of_side] = product

            @pl.when(channel > 0)
            def _():
                products[of_side] += product

        @pl.when(channel == channels - 1)
        def _():
            ahead, behind = quad * PAIR, half // channels * PAIR + quad * PAIR
            group_of = jnp.where(
                later,
                jnp.where(second, group_ref[behind + 1], group_ref[behind]),
                jnp.where(second, group_ref[ahead + 1], group_ref[ahead]),
            )
            coef = [(group_of == group).astype(jnp.float32) for group in range(GROUPS)]

            def gather(index, carry):
                both = [
                    products[of_side, pl.ds(pl.multiple_of(index * rows, rows), rows)]
                    for of_side in range(2)
                ]
                picked = [jnp.where(second, one[events:], one[:events]) for one in both]
                curve = jnp.where(later, picked[1], picked[0])
                for group in range(GROUPS):
                    total[group, index] += curve * coef[group]
                return carry

            lax.fori_loop(0, LAGS, gather, 0, unroll=4)

    lag_up, lag_down = HOP * layer, HOP * (line - 1 - layer)
    lag_out = jnp.maximum(lag_up, lag_down)

    def tick(now):
        @pl.when(now < steps)
        def _():
            beside_copy(now).wait_recv()

        @pl.when(now + AHEAD < steps)
        def _():
            beside_copy(now + AHEAD).start()

        step_up = now - lag_up

        @pl.when(jnp.logical_and(step_up >= 0, step_up < steps))
        def _():
            @pl.when(has_below)
            def _():
                up_copy(step_up).wait_recv()

            @pl.when(has_above)
            def _():
                for slot in range(slots):
                    up_out[step_up, slot] = merged(step_up, slot, up_in[step_up, slot])
                up_copy(step_up).start()

        step_down = now - lag_down

        @pl.when(jnp.logical_and(step_down >= 0, step_down < steps))
        def _():
            @pl.when(has_above)
            def _():
                down_copy(step_down).wait_recv()

            @pl.when(has_below)
            def _():
                for slot in range(slots):
                    down_out[step_down, slot] = merged(step_down, slot, down_in[step_down, slot])
                down_copy(step_down).start()

        step_out = now - lag_out

        @pl.when(jnp.logical_and(step_out >= 0, step_out < steps))
        def _():
            rows = pl.ds(side * half + step_out * CHUNK, CHUNK)
            for slot in range(slots):
                passing = jnp.where(lower[slot], up_in[step_out, slot], down_in[step_out, slot])
                out_ref[slot, rows] = merged(step_out, slot, passing)
            out_copy(step_out, side).start()

        step_curve = step_out - HOP

        @pl.when(jnp.logical_and(step_curve >= 0, step_curve < steps))
        def _():
            out_copy(step_curve, 1 - side).wait_recv()
            each(CHUNK, lambda number: correlate(step_curve * CHUNK + number))

    @pl.when(jnp.logical_not(has_below))
    def _():
        up_in[...] = jnp.zeros_like(up_in)

    @pl.when(jnp.logical_not(has_above))
    def _():
        down_in[...] = jnp.zeros_like(down_in)

    each(steps + HOP * line, tick)

    def finish(step):
        beside_copy(step).wait_send()

        @pl.when(has_above)
        def _():
            up_copy(step).wait_send()

        @pl.when(has_below)
        def _():
            down_copy(step).wait_send()

        out_copy(step, side).wait_send()

    each(steps, finish)
    own_flags.wait()

    def finish_flags(hop):
        flags_copy(hop, tile).wait_send()
        flags_copy(hop, lax.rem(tile + tiles - 1 - hop, tiles)).wait_recv()

    each(tiles - 1, finish_flags)

    quarter = LAGS // 4
    place = (lane // (columns // 2)) * 2 + (lane // events) % PAIR
    flags = [everyone_ref[owners_ref[slot]] for slot in range(slots)]
    flags = jnp.concatenate([one for one in flags for _ in range(PAIR)] * 2, axis=0)
    member = jnp.concatenate(
        [jnp.where(member_ref[...] == group, flags_ref[...], 0.0) for group in range(GROUPS)], axis=0
    )
    common_ref[...] = lax.dot_general(
        member, flags, (((1,), (1,)), ((), ())), preferred_element_type=jnp.float32
    ).reshape(common_ref.shape)

    def pack(group):
        values = total[group].reshape(LAGS * events, columns)
        values = values + pltpu.roll(values, columns // 2, axis=1)
        ahead = pltpu.roll(values, columns - events, axis=1)
        behind = pltpu.roll(values, events, axis=1)
        flag = (lax.broadcasted_iota(jnp.int32, values.shape, 1) // events) % PAIR == 1
        values = (values + jnp.where(flag, behind, ahead)).reshape(LAGS, events, columns)
        packed = values[:quarter]
        for number in range(1, 4):
            packed = jnp.where(
                (place == number)[None], values[number * quarter : (number + 1) * quarter], packed
            )
        part[group] = packed

    copies, counts = [], []
    for hop in range(1, parts + 1):
        target = lax.rem(sta + hop, parts)
        for number in range(share):
            pack(target * share + number)
        if hop == parts:
            break
        theirs = pl.ds(target * share, share)
        for source, place_in, done, came, started in (
            (part, landed, send, recv, copies),
            (common_ref, counted, count_send, count_recv, counts),
        ):
            copy = pltpu.make_async_remote_copy(
                src_ref=source.at[theirs], dst_ref=place_in.at[hop - 1],
                send_sem=done.at[hop - 1], recv_sem=came.at[hop - 1],
                device_id=(tile, target), device_id_type=MESH,
            )
            copy.start()
            started.append(copy)
    ours = pl.ds(sta * share, share)
    common, summed = common_ref[ours], part[ours]
    for hop in range(1, parts):
        copies[hop - 1].wait_recv()
        summed = summed + landed[hop - 1]
    for hop in range(1, parts):
        counts[hop - 1].wait_recv()
        common = common + counted[hop - 1]
    highest = jnp.max(summed, axis=1)
    highest = highest.reshape(share * events, columns)
    highest = jnp.maximum(highest, pltpu.roll(highest, columns // 2, axis=1))
    flag = (lax.broadcasted_iota(jnp.int32, highest.shape, 1) // events) % PAIR == 1
    highest = jnp.maximum(
        highest,
        jnp.where(
            flag, pltpu.roll(highest, events, axis=1), pltpu.roll(highest, columns - events, axis=1)
        ),
    )
    peak_ref[pl.ds(sta * share, share)] = highest.reshape(share, events, columns) / (
        samples * jnp.maximum(common, 1.0)
    )
    backs = []
    for hop in range(1, parts):
        mine = pl.ds(sta * share, share)
        copy = pltpu.make_async_remote_copy(
            src_ref=peak_ref.at[mine], dst_ref=peak_ref.at[mine],
            send_sem=back_send.at[hop - 1], recv_sem=back_recv.at[hop - 1],
            device_id=(tile, lax.rem(sta + hop, parts)), device_id_type=MESH,
        )
        copy.start()
        backs.append(copy)
    for copy in copies + counts:
        copy.wait_send()
    for hop in range(1, parts):
        backs[hop - 1].wait_send()
        theirs = pl.ds(lax.rem(sta + parts - hop, parts) * share, share)
        pltpu.make_async_remote_copy(
            src_ref=peak_ref.at[theirs], dst_ref=peak_ref.at[theirs],
            send_sem=back_send.at[hop - 1], recv_sem=back_recv.at[hop - 1],
            device_id=(tile, lax.rem(sta + hop, parts)), device_id_type=MESH,
        ).wait_recv()


def peaks(owners, station_group, blocks, flags, members, line, parts, samples):
    slots = owners.shape[0]
    count, rows, width = blocks.shape
    events = rows // PAIR
    columns = 2 * slots * rows
    share = GROUPS // parts
    steps = count // 2 // CHUNK
    store = pltpu.VMEM((steps, slots, CHUNK, rows, width), blocks.dtype)
    dma = pltpu.SemaphoreType.DMA((steps,))
    dma_tile = pltpu.SemaphoreType.DMA((2 * line - 1,))
    dma_sta = pltpu.SemaphoreType.DMA((parts - 1,))
    return pl.pallas_call(
        functools.partial(peak_kernel, line, parts, slots, float(samples)),
        out_shape=jax.ShapeDtypeStruct((GROUPS, events, columns), jnp.float32),
        in_specs=[pl.BlockSpec(memory_space=pltpu.SMEM)] * 2
        + [pl.BlockSpec(memory_space=pltpu.VMEM)] * 3,
        out_specs=pl.BlockSpec(memory_space=pltpu.VMEM),
        scratch_shapes=[
            pltpu.VMEM((slots, count, rows, width), blocks.dtype),
            pltpu.VMEM((2 * line,) + flags.shape, flags.dtype),
            pltpu.VMEM((2, LAGS * rows, width), blocks.dtype),
            pltpu.VMEM((2, LAGS * rows, columns), jnp.float32),
            pltpu.VMEM((GROUPS, LAGS, events, columns), jnp.float32),
            pltpu.VMEM((GROUPS, LAGS // 4, events, columns), jnp.float32),
            pltpu.VMEM((parts - 1, share, LAGS // 4, events, columns), jnp.float32),
            pltpu.VMEM((GROUPS, events, columns), jnp.float32),
            pltpu.VMEM((parts - 1, share, events, columns), jnp.float32),
            pltpu.VMEM((steps, CHUNK, rows, width), blocks.dtype), store, store, store, store,
        ]
        + [dma] * 8
        + [dma_tile, dma_tile, pltpu.SemaphoreType.DMA]
        + [dma_sta] * 6,
        compiler_params=pltpu.CompilerParams(
            collective_id=0, has_side_effects=True, vmem_limit_bytes=VMEM_LIMIT
        ),
    )(owners, station_group, blocks, flags, members)


def shards(tiles, parts, waves, valid, station_group, owners):
    stations, events, channels, samples = waves.shape
    slots = owners.shape[0]
    flags = jnp.pad(valid.T.astype(jnp.float32), ((0, 0), (0, -stations % 128)))

    pairs = stations // PAIR
    normed = normalize(waves, valid).reshape(pairs, PAIR, events, channels, samples)
    normed = normed.transpose(0, 3, 1, 2, 4).reshape(pairs * channels, PAIR * events, samples)

    members = jnp.broadcast_to(jnp.pad(station_group, (0, -stations % 128))[None], flags.shape)
    highest = peaks(owners, station_group, normed, flags, members, tiles // 2, parts, samples)
    highest = highest.reshape(GROUPS, events, 2, slots, PAIR, events)[:, :, 0, :, 0, :]
    return highest.reshape(GROUPS, events, slots * events).transpose(0, 2, 1)


def solution(mesh):
    return jax.shard_map(
        functools.partial(shards, mesh.shape["tile"], mesh.shape["sta"]),
        mesh=mesh,
        in_specs=(P("sta", "tile", None, None), P("sta", "tile"), P("sta"), P()),
        out_specs=P(None, None, "tile"),
        check_vma=False,
    )
```

```python
import functools

import jax
import jax.numpy as jnp
from jax import lax
from jax.experimental import pallas as pl
from jax.experimental.pallas import tpu as pltpu
from jax.sharding import PartitionSpec as P

LAGS = 64
GROUPS = 8
PAIR = 2
CHUNK = 1
HOP = 3
AHEAD = 4
epsilon = 1e-06
MESH = pl.DeviceIdType.MESH
VMEM_LIMIT = 56 * 1024 * 1024


def normalize(raw_block, mask_block):
    signal = raw_block.astype(jnp.float32)
    inverse_rms = lax.rsqrt(jnp.mean(signal * signal, axis=-1, keepdims=True) + epsilon)
    return (signal * inverse_rms * mask_block[:, :, None, None].astype(jnp.float32)).astype(
        jnp.bfloat16
    )


def peak_kernel(
    line, parts, slots, samples,
    owners_ref, group_ref, mine_ref, flags_ref, member_ref, peak_ref,
    out_ref, everyone_ref, shifted, products, total, part, landed, common_ref, counted, gathered,
    beside, up_out, up_in, down_out, down_in,
    beside_send, beside_recv, up_send, up_recv, down_send, down_recv, out_send, out_recv,
    flags_send, flags_recv, flags_local,
    send, recv, count_send, count_recv, back_send, back_recv,
):
    tile, sta = lax.axis_index("tile"), lax.axis_index("sta")
    layer, side = tile // 2, tile % 2
    other = layer * 2 + (1 - side)
    half = mine_ref.shape[0] // 2
    steps = half // CHUNK
    above, below = layer * 2 + 2 + side, layer * 2 - 2 + side
    has_above, has_below = layer < line - 1, layer > 0

    tiles = 2 * line

    def each(count, body):
        def run(index, carry):
            body(index)
            return carry

        lax.fori_loop(0, count, run, 0)

    barrier = pltpu.get_barrier_semaphore()
    each(
        tiles - 1,
        lambda hop: pl.semaphore_signal(
            barrier, inc=1, device_id=(lax.rem(tile + 1 + hop, tiles), sta), device_id_type=MESH
        ),
    )
    for hop in range(1, parts):
        pl.semaphore_signal(
            barrier, inc=1, device_id=(tile, lax.rem(sta + hop, parts)), device_id_type=MESH
        )
    pl.semaphore_wait(barrier, tiles - 1 + parts - 1)

    def flags_copy(hop, row):
        return pltpu.make_async_remote_copy(
            src_ref=flags_ref, dst_ref=everyone_ref.at[row],
            send_sem=flags_send.at[hop], recv_sem=flags_recv.at[hop],
            device_id=(lax.rem(tile + 1 + hop, tiles), sta), device_id_type=MESH,
        )

    def beside_copy(step):
        return pltpu.make_async_remote_copy(
            src_ref=mine_ref.at[pl.ds((1 - side) * half + step * CHUNK, CHUNK)],
            dst_ref=beside.at[step],
            send_sem=beside_send.at[step], recv_sem=beside_recv.at[step],
            device_id=(other, sta), device_id_type=MESH,
        )

    def up_copy(step):
        return pltpu.make_async_remote_copy(
            src_ref=up_out.at[step], dst_ref=up_in.at[step],
            send_sem=up_send.at[step], recv_sem=up_recv.at[step],
            device_id=(above, sta), device_id_type=MESH,
        )

    def down_copy(step):
        return pltpu.make_async_remote_copy(
            src_ref=down_out.at[step], dst_ref=down_in.at[step],
            send_sem=down_send.at[step], recv_sem=down_recv.at[step],
            device_id=(below, sta), device_id_type=MESH,
        )

    def out_copy(step, of_side):
        rows = pl.ds(of_side * half + step * CHUNK, CHUNK)
        return pltpu.make_async_remote_copy(
            src_ref=out_ref.at[:, rows], dst_ref=out_ref.at[:, rows],
            send_sem=out_send.at[step], recv_sem=out_recv.at[step],
            device_id=(other, sta), device_id_type=MESH,
        )

    each(AHEAD, lambda step: beside_copy(step).start())
    each(tiles - 1, lambda hop: flags_copy(hop, tile).start())
    own_flags = pltpu.make_async_copy(flags_ref, everyone_ref.at[tile], flags_local)
    own_flags.start()
    own = [owners_ref[slot] == tile for slot in range(slots)]
    near = [owners_ref[slot] == other for slot in range(slots)]
    lower = [owners_ref[slot] < layer * 2 for slot in range(slots)]

    def merged(step, slot, passing):
        local = mine_ref[pl.ds(side * half + step * CHUNK, CHUNK)]
        return jnp.where(own[slot], local, jnp.where(near[slot], beside[step], passing))

    rows, width = mine_ref.shape[-2:]
    events = rows // PAIR
    columns = 2 * slots * rows
    share = GROUPS // parts
    lane = lax.broadcasted_iota(jnp.int32, (events, columns), 1)
    second = (lane // events) % PAIR == 1
    later = lane >= columns // 2
    channels = 2 * half // (group_ref.shape[0] // PAIR)
    total[...] = jnp.zeros_like(total)

    def correlate(step):
        channel, quad = lax.rem(step, channels), step // channels
        queries = jnp.concatenate(
            [out_ref[slot, of_side * half + step] for of_side in range(2) for slot in range(slots)],
            axis=0,
        )
        for of_side in range(2):
            row = mine_ref[of_side * half + step].astype(jnp.float32)
            row = jnp.concatenate([row, jnp.zeros((rows, 128), jnp.float32)], axis=1)
            for index in range(LAGS):
                shift = (index - LAGS // 2) % (width + 128)
                moved = pltpu.roll(row, shift, axis=1) if shift else row
                shifted[of_side, pl.ds(index * rows, rows)] = moved[:, :width].astype(jnp.bfloat16)
            product = lax.dot_general(
                shifted[of_side], queries, (((1,), (1,)), ((), ())),
                preferred_element_type=jnp.float32,
            )

            @pl.when(channel == 0)
            def _():
                products[of_side] = product

            @pl.when(channel > 0)
            def _():
                products[of_side] += product

        @pl.when(channel == channels - 1)
        def _():
            ahead, behind = quad * PAIR, half // channels * PAIR + quad * PAIR
            group_of = jnp.where(
                later,
                jnp.where(second, group_ref[behind + 1], group_ref[behind]),
                jnp.where(second, group_ref[ahead + 1], group_ref[ahead]),
            )
            coef = [(group_of == group).astype(jnp.float32) for group in range(GROUPS)]

            def gather(index, carry):
                both = [
                    products[of_side, pl.ds(pl.multiple_of(index * rows, rows), rows)]
                    for of_side in range(2)
                ]
                picked = [jnp.where(second, one[events:], one[:events]) for one in both]
                curve = jnp.where(later, picked[1], picked[0])
                for group in range(GROUPS):
                    total[group, index] += curve * coef[group]
                return carry

            lax.fori_loop(0, LAGS, gather, 0, unroll=4)

    lag_up, lag_down = HOP * layer, HOP * (line - 1 - layer)
    lag_out = jnp.maximum(lag_up, lag_down)

    def tick(now):
        @pl.when(now < steps)
        def _():
            beside_copy(now).wait_recv()

        @pl.when(now + AHEAD < steps)
        def _():
            beside_copy(now + AHEAD).start()

        step_up = now - lag_up

        @pl.when(jnp.logical_and(step_up >= 0, step_up < steps))
        def _():
            @pl.when(has_below)
            def _():
                up_copy(step_up).wait_recv()

            @pl.when(has_above)
            def _():
                for slot in range(slots):
                    up_out[step_up, slot] = merged(step_up, slot, up_in[step_up, slot])
                up_copy(step_up).start()

        step_down = now - lag_down

        @pl.when(jnp.logical_and(step_down >= 0, step_down < steps))
        def _():
            @pl.when(has_above)
            def _():
                down_copy(step_down).wait_recv()

            @pl.when(has_below)
            def _():
                for slot in range(slots):
                    down_out[step_down, slot] = merged(step_down, slot, down_in[step_down, slot])
                down_copy(step_down).start()

        step_out = now - lag_out

        @pl.when(jnp.logical_and(step_out >= 0, step_out < steps))
        def _():
            rows = pl.ds(side * half + step_out * CHUNK, CHUNK)
            for slot in range(slots):
                passing = jnp.where(lower[slot], up_in[step_out, slot], down_in[step_out, slot])
                out_ref[slot, rows] = merged(step_out, slot, passing)
            out_copy(step_out, side).start()

        step_curve = step_out - HOP

        @pl.when(jnp.logical_and(step_curve >= 0, step_curve < steps))
        def _():
            out_copy(step_curve, 1 - side).wait_recv()
            each(CHUNK, lambda number: correlate(step_curve * CHUNK + number))

    @pl.when(jnp.logical_not(has_below))
    def _():
        up_in[...] = jnp.zeros_like(up_in)

    @pl.when(jnp.logical_not(has_above))
    def _():
        down_in[...] = jnp.zeros_like(down_in)

    each(steps + HOP * line, tick)

    def finish(step):
        beside_copy(step).wait_send()

        @pl.when(has_above)
        def _():
            up_copy(step).wait_send()

        @pl.when(has_below)
        def _():
            down_copy(step).wait_send()

        out_copy(step, side).wait_send()

    each(steps, finish)
    own_flags.wait()

    def finish_flags(hop):
        flags_copy(hop, tile).wait_send()
        flags_copy(hop, lax.rem(tile + tiles - 1 - hop, tiles)).wait_recv()

    each(tiles - 1, finish_flags)

    quarter = LAGS // 4
    place = (lane // (columns // 2)) * 2 + (lane // events) % PAIR
    flags = [everyone_ref[owners_ref[slot]] for slot in range(slots)]
    flags = jnp.concatenate([one for one in flags for _ in range(PAIR)] * 2, axis=0)
    member = jnp.concatenate(
        [jnp.where(member_ref[...] == group, flags_ref[...], 0.0) for group in range(GROUPS)], axis=0
    )
    common_ref[...] = lax.dot_general(
        member, flags, (((1,), (1,)), ((), ())), preferred_element_type=jnp.float32
    ).reshape(common_ref.shape)

    def pack(group):
        values = total[group].reshape(LAGS * events, columns)
        values = values + pltpu.roll(values, columns // 2, axis=1)
        ahead = pltpu.roll(values, columns - events, axis=1)
        behind = pltpu.roll(values, events, axis=1)
        flag = (lax.broadcasted_iota(jnp.int32, values.shape, 1) // events) % PAIR == 1
        values = (values + jnp.where(flag, behind, ahead)).reshape(LAGS, events, columns)
        packed = values[:quarter]
        for number in range(1, 4):
            packed = jnp.where(
                (place == number)[None], values[number * quarter : (number + 1) * quarter], packed
            )
        part[group] = packed

    copies, counts = [], []
    for hop in range(1, parts + 1):
        target = lax.rem(sta + hop, parts)
        for number in range(share):
            pack(target * share + number)
        if hop == parts:
            break
        theirs = pl.ds(target * share, share)
        for source, place_in, done, came, started in (
            (part, landed, send, recv, copies),
            (common_ref, counted, count_send, count_recv, counts),
        ):
            copy = pltpu.make_async_remote_copy(
                src_ref=source.at[theirs], dst_ref=place_in.at[hop - 1],
                send_sem=done.at[hop - 1], recv_sem=came.at[hop - 1],
                device_id=(tile, target), device_id_type=MESH,
            )
            copy.start()
            started.append(copy)
    ours = pl.ds(sta * share, share)
    common, summed = common_ref[ours], part[ours]
    for hop in range(1, parts):
        copies[hop - 1].wait_recv()
        summed = summed + landed[hop - 1]
    for hop in range(1, parts):
        counts[hop - 1].wait_recv()
        common = common + counted[hop - 1]
    highest = jnp.max(summed, axis=1)
    highest = highest.reshape(share * events, columns)
    highest = jnp.maximum(highest, pltpu.roll(highest, columns // 2, axis=1))
    flag = (lax.broadcasted_iota(jnp.int32, highest.shape, 1) // events) % PAIR == 1
    highest = jnp.maximum(
        highest,
        jnp.where(
            flag, pltpu.roll(highest, events, axis=1), pltpu.roll(highest, columns - events, axis=1)
        ),
    )
    gathered[pl.ds(sta * share, share)] = highest.reshape(share, events, columns) / (
        samples * jnp.maximum(common, 1.0)
    )
    backs = []
    for hop in range(1, parts):
        mine = pl.ds(sta * share, share)
        copy = pltpu.make_async_remote_copy(
            src_ref=gathered.at[mine], dst_ref=gathered.at[mine],
            send_sem=back_send.at[hop - 1], recv_sem=back_recv.at[hop - 1],
            device_id=(tile, lax.rem(sta + hop, parts)), device_id_type=MESH,
        )
        copy.start()
        backs.append(copy)
    for copy in copies + counts:
        copy.wait_send()
    for hop in range(1, parts):
        backs[hop - 1].wait_send()
        theirs = pl.ds(lax.rem(sta + parts - hop, parts) * share, share)
        pltpu.make_async_remote_copy(
            src_ref=gathered.at[theirs], dst_ref=gathered.at[theirs],
            send_sem=back_send.at[hop - 1], recv_sem=back_recv.at[hop - 1],
            device_id=(tile, lax.rem(sta + hop, parts)), device_id_type=MESH,
        ).wait_recv()
    for group in range(GROUPS):
        turned = jnp.transpose(gathered[group])
        for slot in range(slots):
            peak_ref[group, pl.ds(slot * events, events)] = (
                turned[slot * rows : slot * rows + events]
            )


def peaks(owners, station_group, blocks, flags, members, line, parts, samples):
    slots = owners.shape[0]
    count, rows, width = blocks.shape
    events = rows // PAIR
    columns = 2 * slots * rows
    share = GROUPS // parts
    steps = count // 2 // CHUNK
    store = pltpu.VMEM((steps, slots, CHUNK, rows, width), blocks.dtype)
    dma = pltpu.SemaphoreType.DMA((steps,))
    dma_tile = pltpu.SemaphoreType.DMA((2 * line - 1,))
    dma_sta = pltpu.SemaphoreType.DMA((parts - 1,))
    return pl.pallas_call(
        functools.partial(peak_kernel, line, parts, slots, float(samples)),
        out_shape=jax.ShapeDtypeStruct((GROUPS, slots * events, events), jnp.float32),
        in_specs=[pl.BlockSpec(memory_space=pltpu.SMEM)] * 2
        + [pl.BlockSpec(memory_space=pltpu.VMEM)] * 3,
        out_specs=pl.BlockSpec(memory_space=pltpu.VMEM),
        scratch_shapes=[
            pltpu.VMEM((slots, count, rows, width), blocks.dtype),
            pltpu.VMEM((2 * line,) + flags.shape, flags.dtype),
            pltpu.VMEM((2, LAGS * rows, width), blocks.dtype),
            pltpu.VMEM((2, LAGS * rows, columns), jnp.float32),
            pltpu.VMEM((GROUPS, LAGS, events, columns), jnp.float32),
            pltpu.VMEM((GROUPS, LAGS // 4, events, columns), jnp.float32),
            pltpu.VMEM((parts - 1, share, LAGS // 4, events, columns), jnp.float32),
            pltpu.VMEM((GROUPS, events, columns), jnp.float32),
            pltpu.VMEM((parts - 1, share, events, columns), jnp.float32),
            pltpu.VMEM((GROUPS, events, columns), jnp.float32),
            pltpu.VMEM((steps, CHUNK, rows, width), blocks.dtype), store, store, store, store,
        ]
        + [dma] * 8
        + [dma_tile, dma_tile, pltpu.SemaphoreType.DMA]
        + [dma_sta] * 6,
        compiler_params=pltpu.CompilerParams(
            collective_id=0, has_side_effects=True, vmem_limit_bytes=VMEM_LIMIT
        ),
    )(owners, station_group, blocks, flags, members)


def shards(tiles, parts, waves, valid, station_group, owners):
    stations, events, channels, samples = waves.shape
    slots = owners.shape[0]
    flags = jnp.pad(valid.T.astype(jnp.float32), ((0, 0), (0, -stations % 128)))

    pairs = stations // PAIR
    normed = normalize(waves, valid).reshape(pairs, PAIR, events, channels, samples)
    normed = normed.transpose(0, 3, 1, 2, 4).reshape(pairs * channels, PAIR * events, samples)

    members = jnp.broadcast_to(jnp.pad(station_group, (0, -stations % 128))[None], flags.shape)
    return peaks(
        owners, station_group, normed, flags, members, tiles // 2, parts, samples
    )


def solution(mesh):
    return jax.shard_map(
        functools.partial(shards, mesh.shape["tile"], mesh.shape["sta"]),
        mesh=mesh,
        in_specs=(P("sta", "tile", None, None), P("sta", "tile"), P("sta"), P()),
        out_specs=P(None, None, "tile"),
        check_vma=False,
    )
```
